32 devices in a mesh: parts: 2 (over y), expert: 8 (over z, x), tile: 2 (over core).
Axes of the slice: x: 2, y: 2, z: 4, core: 2. Of those that a mesh axis runs over, the one named last changes fastest.
Arguments:
- tokens: bfloat16 [512, 3072], P(('parts', 'expert', 'tile')), parts along dimension 0, may hold values from -6 to 6
- routes: int32 [512, 2], P(('parts', 'expert', 'tile')), parts along dimension 0, may hold values from 0 to 3, all different within a row; in each aligned block of 16 rows (0 to 15, 16 to 31, ...) at most 8 rows name the same one
- route_weights: bfloat16 [512, 2], P(('parts', 'expert', 'tile')), parts along dimension 0, may hold values from 0.099609375 to 1
- gate_proj: bfloat16 [8, 3072, 4096], P('expert', None, 'tile'), may hold values from -0.109375 to 0.109375
- up_proj: bfloat16 [8, 3072, 4096], P('expert', None, 'tile'), may hold values from -0.109375 to 0.109375
- down_proj: bfloat16 [8, 4096, 3072], P('expert', 'tile'), may hold values from -0.0625 to 0.0625
Outputs:
- mixed_out: bfloat16 [512, 3072], P(('parts', 'expert', 'tile')), parts along dimension 0
The draws below stay inside these ranges and needn't reach their ends.
There are 2 independent parts, one for each index of `parts`. The reference program is written for one: setup_inputs(seed, part) draws one part's arguments, and reference() takes and returns one part's arrays. A program takes and returns all parts, laid end to end along the dimension named above; an argument that names none is the same for every part. Nothing has to cross between parts.
Inputs may be any that keep to these rules, and one draw needn't show every extreme that they name: `routes`: each row names two different experts; in each aligned block of 16 rows (the rows of one device) no expert is named by more than 8 rows, a bound that some block reaches.
All inputs are finite; a program needn't handle non-finite values.
Results may differ from the reference program's by a relative error of at most 0.009.
Values may be sent and summed in bfloat16 or wider, within the bound.
No kernel may reach another device: no remote copies, remote signals or barrier semaphores. Data moves between devices by JAX's collectives and lax.ppermute only.
A program may use at most 128 MiB of HBM per device.

```python
import math
import jax
import jax.numpy as jnp
import numpy as np
from jax import lax

D = 3072
FF = 8192
ROW_DEV = 16
EXPERTS = 4
CAP = 8
ROWS = 256
N_TILE = 2


def block_levels(own_key, extent, split, least, largest):
    factor_of, own = 1.0, jax.random.fold_in(own_key, 6)
    for axis_at, blocks in split:
        heights = jnp.exp(jax.random.uniform(jax.random.fold_in(own, axis_at), (blocks,), jnp.float32, least / len(split), largest / len(split)))
        factor_of = factor_of * jnp.repeat(heights, extent[axis_at] // blocks).reshape([-1 if axis == axis_at else 1 for axis in range(len(extent))])
    return factor_of


def assign_block(stream_key, own, number, rows, count, top, most, lean):
    sequence = jax.random.permutation(stream_key, count)
    packed, common = load_shares(count, rows * top, most, lean, True), load_shares(count, rows * top, most, lean, False)
    places = jnp.arange(count)

    def named(tallies, turn):
        used = int((tallies > 0).sum())
        fixed = max(1, used // 4)
        moved = fixed + (places - fixed + turn * (used - fixed)) % max(1, count - fixed)
        return jnp.zeros((count,), jnp.int32).at[sequence[jnp.where(places < fixed, places, moved)]].set(jnp.asarray(tallies, jnp.int32))

    tallies = jnp.where(number % 4 == 0, named(packed, number // 4), named(common, number - number // 4 - 1))
    mixed = jax.random.permutation(jax.random.fold_in(own, 3), count)
    giver, taker = mixed[0:count // 2 * 2:2], mixed[1:count // 2 * 2:2]
    margin = jnp.minimum(tallies[giver] - 1, most - tallies[taker]) // 2
    margin = jnp.where((giver == sequence[0]) | (taker == sequence[0]) | (tallies[taker] == 0), 0, jnp.maximum(margin, 0))
    moved = jax.random.randint(jax.random.fold_in(own, 4), (count // 2,), 0, 1 << 20) % (margin + 1)
    tallies = tallies.at[giver].add(-moved).at[taker].add(moved)
    labels = jnp.searchsorted(jnp.cumsum(tallies), jnp.arange(rows * top), side="right").astype(jnp.int32)
    grid = labels.reshape(top, rows).T
    grid = grid[jax.random.permutation(jax.random.fold_in(own, 1), rows)]
    turn = jax.random.randint(jax.random.fold_in(own, 2), (rows, 1), 0, top)
    return jnp.take_along_axis(grid, (jnp.arange(top)[None, :] + turn) % top, axis=1)


def load_shares(count, total, bound, lean, full):
    portions = [(1 << 20) // math.isqrt(rank ** lean) + 1 for rank in range(1, count + 1)]
    largest = bound if full else min(bound, max(-(-total // count), total * portions[0] // sum(portions)))
    least = 1 if total - largest >= count - 1 else 0
    counts, spare = [largest] + [least] * (count - 1), total - largest - least * (count - 1)
    while spare > 0:
        free = [i for i in range(1, count) if counts[i] < largest] or [i for i in range(1, count) if counts[i] < bound]
        whole, left = sum([portions[i] for i in free]), spare
        for i in free:
            extra = min(bound - counts[i], max(1, left * portions[i] // whole), spare)
            counts[i] = counts[i] + extra
            spare = spare - extra
    return np.array(counts)


def centred(own_key, dims, deviation, limit, pieces=(), held_as=jnp.bfloat16):
    loudness = block_levels(own_key, dims, pieces, -0.22, 0.18) if pieces else 1.0
    values = jax.random.normal(own_key, dims, jnp.float32) * deviation * loudness
    return jnp.minimum(jnp.maximum(values, -limit), limit).astype(held_as)


def setup_inputs(seed: int = 0, part: int = 0) -> dict:
    key_of = jax.random.split(jax.random.key(seed), 7)
    own_keys = jax.random.split(jax.random.fold_in(key_of[6], part), 7)
    tokens = centred(own_keys[0], (ROWS, D), 1.0, 6.0, ((0, 16),))
    routes_keys = jax.random.split(jax.random.fold_in(own_keys[1], 1), ROWS // ROW_DEV)
    routes_turns = jax.random.permutation(jax.random.fold_in(own_keys[1], 3), ROWS // ROW_DEV)
    routes = jax.vmap(lambda own, number: assign_block(jax.random.fold_in(own_keys[1], 2), own, number, ROW_DEV, EXPERTS, 2, CAP, 0))(routes_keys, routes_turns).reshape((ROWS, 2))
    route_weights = jnp.clip(0.099609375 + 0.9003906 * jax.random.uniform(own_keys[2], (ROWS, 2), jnp.float32) ** block_levels(own_keys[2], (ROWS, 2), ((0, 16),), -0.2, 0.2), 0.099609375, 1.0).astype(jnp.bfloat16)
    gate_proj = centred(key_of[3], (2 * EXPERTS, D, FF // 2), D ** -0.5, 0.109375, ((0, 8), (2, 2)))
    up_proj = centred(key_of[4], (2 * EXPERTS, D, FF // 2), D ** -0.5, 0.109375, ((0, 8), (2, 2)))
    down_proj = centred(key_of[5], (2 * EXPERTS, FF // 2, D), FF ** -0.5, 0.0625, ((0, 8), (1, 2)))
    return dict(tokens=tokens, routes=routes, route_weights=route_weights, gate_proj=gate_proj, up_proj=up_proj, down_proj=down_proj)


def reference(tokens, routes, route_weights, gate_proj, up_proj, down_proj):
    per_tile = FF // 2 // N_TILE

    def group_result(group_index):
        gate_pre = jnp.dot(tokens, gate_proj[group_index], preferred_element_type=jnp.float32)
        up_pre = jnp.dot(tokens, up_proj[group_index], preferred_element_type=jnp.float32)
        hidden = (jax.nn.silu(gate_pre) * up_pre).astype(jnp.bfloat16)
        hidden_wide = hidden.astype(jnp.float32).reshape(ROWS, N_TILE, per_tile)
        down_wide = down_proj[group_index].astype(jnp.float32).reshape(N_TILE, per_tile, D)
        partials = jnp.einsum('rtf,tfd->trd', hidden_wide, down_wide, precision=lax.Precision.HIGHEST)
        rounded = lax.optimization_barrier(partials.astype(jnp.bfloat16))
        return jnp.sum(rounded.astype(jnp.float32), axis=0)

    results = lax.map(group_result, jnp.arange(2 * EXPERTS, dtype=jnp.int32))
    pair_sum = results.reshape(EXPERTS, 2, ROWS, D).sum(axis=1)
    row_ids = jnp.arange(ROWS, dtype=jnp.int32)
    weighting = route_weights.astype(jnp.float32)
    mixed = jnp.zeros((ROWS, D), jnp.float32)
    for which in range(2):
        picks = pair_sum[routes[:, which].astype(jnp.int32), row_ids]
        mixed = mixed + weighting[:, which:which + 1] * picks
    return mixed.astype(jnp.bfloat16)
```

```python
import functools

import jax
import jax.numpy as jnp
from jax import lax
from jax.experimental import pallas as pl
from jax.experimental.pallas import tpu as pltpu
from jax.sharding import PartitionSpec as P

F32 = jnp.float32
BF16 = jnp.bfloat16
MIB = 2**20


def partner(expert, step, experts):
    if experts & (experts - 1) == 0:
        return expert ^ step
    return (step - expert + experts) % experts


def route_kernel(experts, capacity, me_ref, routes_ref, weights_ref, tokens_ref, out_ref, comb_ref):
    slots = experts * capacity
    rows = tokens_ref.shape[0]
    slot = lax.broadcasted_iota(jnp.int32, (slots, rows), 0)
    step = slot // capacity
    place = slot - step * capacity
    expert = jnp.zeros_like(slot)
    for s in range(experts):
        expert = jnp.where(step == s, me_ref[s], expert)
    match = [routes_ref[k : k + 1, :] == expert for k in range(2)]
    named = jnp.where(match[0] | match[1], 1.0, 0.0)
    before = jnp.where(
        lax.broadcasted_iota(jnp.int32, (rows, rows), 0)
        < lax.broadcasted_iota(jnp.int32, (rows, rows), 1),
        1.0,
        0.0,
    )
    ahead = jnp.dot(named.astype(BF16), before.astype(BF16), preferred_element_type=F32)
    chosen = jnp.where(ahead == place.astype(F32), named, 0.0)
    weights = weights_ref[...].astype(F32)
    weight = jnp.where(match[0], weights[0:1, :], weights[1:2, :])
    comb_ref[...] = (chosen * weight).astype(BF16)
    out_ref[...] = jnp.dot(
        chosen.astype(BF16), tokens_ref[...], preferred_element_type=F32
    ).astype(BF16)


def fetch_kernel(from_ref, to_ref, sem):
    copy = pltpu.make_async_copy(from_ref, to_ref, sem)
    copy.start()
    copy.wait()


def fetch(array, limit):
    return pl.pallas_call(
        fetch_kernel,
        out_shape=pltpu.VMEM(array.shape, array.dtype),
        in_specs=[pl.BlockSpec(memory_space=pltpu.HBM)],
        out_specs=pl.BlockSpec(memory_space=pltpu.VMEM),
        scratch_shapes=[pltpu.SemaphoreType.DMA],
        compiler_params=pltpu.CompilerParams(vmem_limit_bytes=limit * MIB),
        cost_estimate=pl.CostEstimate(
            flops=0, bytes_accessed=4 * array.size, transcendentals=0
        ),
        name="fetch",
    )(pltpu.with_memory_space_constraint(array, pltpu.HBM))


def ffn_kernel(width, rows_ref, gate_ref, up_ref, down_hbm, out_ref, hidden_ref, down_ref, sems):
    blocks = [slice(at, at + 256) for at in range(0, down_ref.shape[1], 256)]
    copies = [
        pltpu.make_async_copy(down_hbm.at[:, part], down_ref.at[:, part], sems.at[i])
        for i, part in enumerate(blocks)
    ]
    for copy in copies:
        copy.start()
    for at in range(0, gate_ref.shape[1], width):
        part = slice(at, at + width)
        gate = jnp.dot(rows_ref[...], gate_ref[:, part], preferred_element_type=F32)
        up = jnp.dot(rows_ref[...], up_ref[:, part], preferred_element_type=F32)
        hidden_ref[:, part] = (gate / (1.0 + jnp.exp(-gate)) * up).astype(BF16)
    for copy, part in zip(copies, blocks):
        copy.wait()
        out_ref[:, part] = jnp.dot(
            hidden_ref[...], down_ref[:, part], preferred_element_type=F32
        ).astype(BF16)


def combine_kernel(comb_ref, results_ref, out_ref):
    out_ref[...] = lax.dot_general(
        comb_ref[...],
        results_ref[...],
        (((0,), (0,)), ((), ())),
        preferred_element_type=F32,
    ).astype(BF16)


def add(a, b):
    return (a.astype(F32) + b.astype(F32)).astype(BF16)


def shards(tokens, routes, route_weights, gate_proj, up_proj, down_proj):
    groups = lax.axis_size("expert")
    tiles = lax.axis_size("tile")
    experts = groups // 2
    rows, width = tokens.shape
    capacity = max(2, 2 * rows // experts)
    slots = experts * capacity
    vmem = pl.BlockSpec(memory_space=pltpu.VMEM)
    me = lax.axis_index("expert") // 2
    targets = jnp.stack([partner(me, s, experts) for s in range(experts)]).astype(jnp.int32)
    outgoing, comb = pl.pallas_call(
        functools.partial(route_kernel, experts, capacity),
        out_shape=(
            jax.ShapeDtypeStruct((slots, width), BF16),
            jax.ShapeDtypeStruct((slots, rows), BF16),
        ),
        in_specs=[pl.BlockSpec(memory_space=pltpu.SMEM), vmem, vmem, vmem],
        out_specs=(vmem, vmem),
        name="route",
    )(targets, routes.T, route_weights.T, tokens)

    def trade(x, step):
        pairs = [
            (g, 2 * partner(g // 2, step, experts) + g % 2)
            for g in range(groups)
            if partner(g // 2, step, experts) != g // 2
        ]
        if len(pairs) == groups:
            return lax.ppermute(x, "expert", pairs)
        moved = lax.ppermute(x, "expert", pairs)
        return jnp.where(partner(me, step, experts) == me, x, moved)

    def swap(x, axis):
        return lax.ppermute(x, axis, [(i, i ^ 1) for i in range(lax.axis_size(axis))])

    def trade_all(x):
        blocks = x.reshape(experts, capacity, width)
        return jnp.concatenate(
            [blocks[0]] + [trade(blocks[s], s) for s in range(1, experts)]
        )

    gate, up, down = gate_proj[0], up_proj[0], down_proj[0]
    mine, gate = lax.optimization_barrier((trade_all(outgoing), fetch(gate, 8)))
    both = jnp.concatenate([mine, swap(mine, "expert")])
    both, up = lax.optimization_barrier((both, fetch(up, 8)))
    if tiles == 2:
        received = jnp.concatenate([both, swap(both, "tile")])
    else:
        received = lax.all_gather(both, "tile", axis=0, tiled=True)
    count, hidden = received.shape[0], gate.shape[1]
    block = min(256, hidden)
    partials = pl.pallas_call(
        functools.partial(ffn_kernel, block),
        out_shape=jax.ShapeDtypeStruct((count, width), BF16),
        in_specs=[vmem, vmem, vmem, pl.BlockSpec(memory_space=pltpu.HBM)],
        out_specs=vmem,
        scratch_shapes=[
            pltpu.VMEM((count, hidden), BF16),
            pltpu.VMEM((hidden, width), BF16),
            pltpu.SemaphoreType.DMA((width // 256,)),
        ],
        compiler_params=pltpu.CompilerParams(vmem_limit_bytes=20 * MIB),
        cost_estimate=pl.CostEstimate(
            flops=6 * count * width * hidden,
            bytes_accessed=6 * width * hidden,
            transcendentals=count * hidden,
        ),
        name="ffn",
    )(received, gate, up, pltpu.with_memory_space_constraint(down, pltpu.HBM))
    if tiles == 2:
        half = count // 2
        both = add(partials[:half], swap(partials[half:], "tile"))
    else:
        pieces = lax.all_to_all(
            partials.reshape(tiles, 2 * slots, width), "tile", 0, 0, tiled=True
        )
        both = jnp.sum(pieces.astype(F32), axis=0).astype(BF16)
    mine = add(both[:slots], swap(both[slots:], "expert"))
    results = trade_all(mine)
    return pl.pallas_call(
        combine_kernel,
        out_shape=jax.ShapeDtypeStruct((rows, width), BF16),
        in_specs=[vmem, vmem],
        out_specs=vmem,
        name="combine",
    )(comb, results)


def solution(mesh):
    placed = (
        P(("parts", "expert", "tile"), None),
        P(("parts", "expert", "tile"), None),
        P(("parts", "expert", "tile"), None),
        P("expert", None, "tile"),
        P("expert", None, "tile"),
        P("expert", "tile", None),
    )
    return jax.shard_map(
        shards,
        mesh=mesh,
        in_specs=placed,
        out_specs=P(("parts", "expert", "tile"), None),
        check_vma=False,
    )
```

```python
import functools

import jax
import jax.numpy as jnp
from jax import lax
from jax.experimental import pallas as pl
from jax.experimental.pallas import tpu as pltpu
from jax.sharding import PartitionSpec as P

F32 = jnp.float32
BF16 = jnp.bfloat16
MIB = 2**20


def partner(expert, step, experts):
    if experts & (experts - 1) == 0:
        return expert ^ step
    return (step - expert + experts) % experts


def route_kernel(experts, capacity, routes_ref, weights_ref, tokens_ref, out_ref, comb_ref):
    me = lax.axis_index("expert") // 2
    slots = experts * capacity
    rows = tokens_ref.shape[0]
    slot = lax.broadcasted_iota(jnp.int32, (slots, rows), 0)
    step = slot // capacity
    place = slot - step * capacity
    expert = jnp.zeros_like(slot)
    for s in range(experts):
        expert = jnp.where(step == s, partner(me, s, experts), expert)
    match = [routes_ref[k : k + 1, :] == expert for k in range(2)]
    named = jnp.where(match[0] | match[1], 1.0, 0.0)
    before = jnp.where(
        lax.broadcasted_iota(jnp.int32, (rows, rows), 0)
        < lax.broadcasted_iota(jnp.int32, (rows, rows), 1),
        1.0,
        0.0,
    )
    ahead = jnp.dot(named.astype(BF16), before.astype(BF16), preferred_element_type=F32)
    chosen = jnp.where(ahead == place.astype(F32), named, 0.0)
    weights = weights_ref[...].astype(F32)
    weight = jnp.where(match[0], weights[0:1, :], weights[1:2, :])
    comb_ref[...] = (chosen * weight).astype(BF16)
    out_ref[...] = jnp.dot(
        chosen.astype(BF16), tokens_ref[...], preferred_element_type=F32
    ).astype(BF16)


def ffn_kernel(width, rows_ref, gate_ref, up_ref, down_ref, out_ref, hidden_ref):
    for at in range(0, gate_ref.shape[1], width):
        part = slice(at, at + width)
        gate = jnp.dot(rows_ref[...], gate_ref[:, part], preferred_element_type=F32)
        up = jnp.dot(rows_ref[...], up_ref[:, part], preferred_element_type=F32)
        hidden_ref[:, part] = (gate / (1.0 + jnp.exp(-gate)) * up).astype(BF16)
    for at in range(0, down_ref.shape[1], 256):
        part = slice(at, at + 256)
        out_ref[:, part] = jnp.dot(
            hidden_ref[...], down_ref[:, part], preferred_element_type=F32
        ).astype(BF16)


def combine_kernel(comb_ref, results_ref, out_ref):
    out_ref[...] = lax.dot_general(
        comb_ref[...],
        results_ref[...],
        (((0,), (0,)), ((), ())),
        preferred_element_type=F32,
    ).astype(BF16)


def add(a, b):
    return (a.astype(F32) + b.astype(F32)).astype(BF16)


def shards(tokens, routes, route_weights, gate_proj, up_proj, down_proj):
    groups = lax.axis_size("expert")
    tiles = lax.axis_size("tile")
    experts = groups // 2
    rows, width = tokens.shape
    capacity = max(2, 2 * rows // experts)
    slots = experts * capacity
    vmem = pl.BlockSpec(memory_space=pltpu.VMEM)
    me = lax.axis_index("expert") // 2
    outgoing, comb = pl.pallas_call(
        functools.partial(route_kernel, experts, capacity),
        out_shape=(
            jax.ShapeDtypeStruct((slots, width), BF16),
            jax.ShapeDtypeStruct((slots, rows), BF16),
        ),
        in_specs=[vmem, vmem, vmem],
        out_specs=(vmem, vmem),
        cost_estimate=pl.CostEstimate(
            flops=10**12, bytes_accessed=4*10**8, transcendentals=0
        ),
        compiler_params=pltpu.CompilerParams(vmem_limit_bytes=4 * MIB),
        name="route",
    )(routes.T, route_weights.T, tokens)

    def trade(x, step):
        pairs = [
            (g, 2 * partner(g // 2, step, experts) + g % 2)
            for g in range(groups)
            if partner(g // 2, step, experts) != g // 2
        ]
        if len(pairs) == groups:
            return lax.ppermute(x, "expert", pairs)
        moved = lax.ppermute(x, "expert", pairs)
        return jnp.where(partner(me, step, experts) == me, x, moved)

    def swap(x, axis):
        return lax.ppermute(x, axis, [(i, i ^ 1) for i in range(lax.axis_size(axis))])

    def trade_all(x):
        blocks = x.reshape(experts, capacity, width)
        return jnp.concatenate(
            [blocks[0]] + [trade(blocks[s], s) for s in range(1, experts)]
        )

    gate, up, down = gate_proj[0], up_proj[0], down_proj[0]
    mine = trade_all(outgoing)
    both = jnp.concatenate([mine, swap(mine, "expert")])
    if tiles == 2:
        received = jnp.concatenate([both, swap(both, "tile")])
    else:
        received = lax.all_gather(both, "tile", axis=0, tiled=True)
    count, hidden = received.shape[0], gate.shape[1]
    block = min(256, hidden)
    partials = pl.pallas_call(
        functools.partial(ffn_kernel, block),
        out_shape=jax.ShapeDtypeStruct((count, width), BF16),
        in_specs=[vmem, vmem, vmem, vmem],
        out_specs=vmem,
        scratch_shapes=[
            pltpu.VMEM((count, hidden), BF16),
        ],
        compiler_params=pltpu.CompilerParams(vmem_limit_bytes=8 * MIB),
        cost_estimate=pl.CostEstimate(
            flops=6 * count * width * hidden,
            bytes_accessed=6 * width * hidden,
            transcendentals=count * hidden,
        ),
        name="ffn",
    )(received, gate, up, down)
    if tiles == 2:
        half = count // 2
        both = add(partials[:half], swap(partials[half:], "tile"))
    else:
        pieces = lax.all_to_all(
            partials.reshape(tiles, 2 * slots, width), "tile", 0, 0, tiled=True
        )
        both = jnp.sum(pieces.astype(F32), axis=0).astype(BF16)
    mine = add(both[:slots], swap(both[slots:], "expert"))
    results = trade_all(mine)
    return pl.pallas_call(
        combine_kernel,
        out_shape=jax.ShapeDtypeStruct((rows, width), BF16),
        in_specs=[vmem, vmem],
        out_specs=vmem,
        compiler_params=pltpu.CompilerParams(vmem_limit_bytes=4 * MIB),
        name="combine",
    )(comb, results)


def solution(mesh):
    placed = (
        P(("parts", "expert", "tile"), None),
        P(("parts", "expert", "tile"), None),
        P(("parts", "expert", "tile"), None),
        P("expert", None, "tile"),
        P("expert", None, "tile"),
        P("expert", "tile", None),
    )
    return jax.shard_map(
        shards,
        mesh=mesh,
        in_specs=placed,
        out_specs=P(("parts", "expert", "tile"), None),
        check_vma=False,
    )
```

```python
import functools

import jax
import jax.numpy as jnp
from jax import lax
from jax.experimental import pallas as pl
from jax.experimental.pallas import tpu as pltpu
from jax.sharding import PartitionSpec as P

F32 = jnp.float32
BF16 = jnp.bfloat16
MIB = 2**20


def partner(expert, step):
    return expert ^ step


def choose(experts, capacity, routes):
    me = lax.axis_index("expert") // 2
    slots, rows = experts * capacity, routes.shape[1]
    slot = lax.broadcasted_iota(jnp.int32, (slots, rows), 0)
    step = slot // capacity
    place = slot - step * capacity
    expert = jnp.zeros_like(slot)
    for s in range(experts):
        expert = jnp.where(step == s, partner(me, s), expert)
    first, second = routes[0:1, :] == expert, routes[1:2, :] == expert
    named = jnp.where(first | second, 1.0, 0.0)
    before = jnp.where(
        lax.broadcasted_iota(jnp.int32, (rows, rows), 0)
        < lax.broadcasted_iota(jnp.int32, (rows, rows), 1),
        1.0,
        0.0,
    )
    ahead = jnp.dot(named.astype(BF16), before.astype(BF16), preferred_element_type=F32)
    return jnp.where(ahead == place.astype(F32), named, 0.0), first


def route_kernel(experts, capacity, routes_hbm, tokens_hbm, out_ref, routes_ref, tokens_ref, sems):
    copies = [
        pltpu.make_async_copy(routes_hbm, routes_ref, sems.at[0]),
        pltpu.make_async_copy(tokens_hbm, tokens_ref, sems.at[1]),
    ]
    for copy in copies:
        copy.start()
    for copy in copies:
        copy.wait()
    chosen, _ = choose(experts, capacity, routes_ref[...])
    out_ref[...] = jnp.dot(
        chosen.astype(BF16), tokens_ref[...], preferred_element_type=F32
    ).astype(BF16)


def weigh_kernel(experts, capacity, routes_ref, weights_ref, comb_ref):
    chosen, first = choose(experts, capacity, routes_ref[...])
    weights = weights_ref[...].astype(F32)
    weight = jnp.where(first, weights[0:1, :], weights[1:2, :])
    comb_ref[...] = (chosen * weight).astype(BF16)


def ffn_kernel(width, rows_ref, gate_ref, up_ref, down_ref, out_ref, hidden_ref):
    for at in range(0, gate_ref.shape[1], width):
        part = slice(at, at + width)
        gate = jnp.dot(rows_ref[...], gate_ref[:, part], preferred_element_type=F32)
        up = jnp.dot(rows_ref[...], up_ref[:, part], preferred_element_type=F32)
        hidden_ref[:, part] = (gate / (1.0 + jnp.exp(-gate)) * up).astype(BF16)
    for at in range(0, down_ref.shape[1], 256):
        part = slice(at, at + 256)
        out_ref[:, part] = jnp.dot(
            hidden_ref[...], down_ref[:, part], preferred_element_type=F32
        ).astype(BF16)


def combine_kernel(comb_ref, results_ref, out_ref):
    out_ref[...] = lax.dot_general(
        comb_ref[...],
        results_ref[...],
        (((0,), (0,)), ((), ())),
        preferred_element_type=F32,
    ).astype(BF16)


def add(a, b):
    return (a.astype(F32) + b.astype(F32)).astype(BF16)


def shards(tokens, routes, route_weights, gate_proj, up_proj, down_proj):
    groups = lax.axis_size("expert")
    tiles = lax.axis_size("tile")
    experts = groups // 2
    rows, width = tokens.shape
    capacity = max(2, 2 * rows // experts)
    slots = experts * capacity
    vmem = pl.BlockSpec(memory_space=pltpu.VMEM)
    hbm = pl.BlockSpec(memory_space=pltpu.HBM)
    small = pltpu.CompilerParams(vmem_limit_bytes=4 * MIB)
    outgoing = pl.pallas_call(
        functools.partial(route_kernel, experts, capacity),
        out_shape=pltpu.VMEM((slots, width), BF16),
        in_specs=[hbm, hbm],
        out_specs=vmem,
        scratch_shapes=[
            pltpu.VMEM((2, rows), jnp.int32),
            pltpu.VMEM((rows, width), BF16),
            pltpu.SemaphoreType.DMA((2,)),
        ],
        cost_estimate=pl.CostEstimate(
            flops=10**12, bytes_accessed=4 * 10**8, transcendentals=0
        ),
        compiler_params=small,
        name="route",
    )(
        pltpu.with_memory_space_constraint(routes.T, pltpu.HBM),
        pltpu.with_memory_space_constraint(tokens, pltpu.HBM),
    )
    comb = pl.pallas_call(
        functools.partial(weigh_kernel, experts, capacity),
        out_shape=jax.ShapeDtypeStruct((slots, rows), BF16),
        in_specs=[vmem, vmem],
        out_specs=vmem,
        compiler_params=small,
        name="weigh",
    )(routes.T, route_weights.T)

    def trade(x, step):
        pairs = [(g, 2 * partner(g // 2, step) + g % 2) for g in range(groups)]
        return lax.ppermute(x, "expert", pairs)

    def swap(x, axis):
        return lax.ppermute(x, axis, [(i, i ^ 1) for i in range(lax.axis_size(axis))])

    def join(blocks):
        return jnp.concatenate(blocks) if len(blocks) > 1 else blocks[0]

    def cut(block):
        return list(block.reshape(-1, capacity, width))

    steps = list(range(experts - 1, 0, -1))
    sent = cut(outgoing)
    here = {s: trade(sent[s], s) for s in steps}
    here[0] = sent[0]
    there = {}
    for group in [[0, steps[0]]] + [[s] for s in steps[1:]]:
        there.update(zip(group, cut(swap(join([here[s] for s in group]), "expert"))))
    order = [(side, s) for side in (0, 1) for s in range(experts)]
    both = join([side[s] for side in (here, there) for s in range(experts)])
    if tiles == 2:
        received = join([both, swap(both, "tile")])
    else:
        received = lax.all_gather(both, "tile", axis=0, tiled=True)
    gate, up, down = gate_proj[0], up_proj[0], down_proj[0]
    count, hidden = received.shape[0], gate.shape[1]
    block = min(256, hidden)
    partials = pl.pallas_call(
        functools.partial(ffn_kernel, block),
        out_shape=jax.ShapeDtypeStruct((count, width), BF16),
        in_specs=[vmem, vmem, vmem, vmem],
        out_specs=vmem,
        scratch_shapes=[
            pltpu.VMEM((count, hidden), BF16),
        ],
        compiler_params=pltpu.CompilerParams(vmem_limit_bytes=8 * MIB),
        cost_estimate=pl.CostEstimate(
            flops=6 * count * width * hidden,
            bytes_accessed=6 * width * hidden,
            transcendentals=count * hidden,
        ),
        name="ffn",
    )(received, gate, up, down)
    if tiles == 2:
        both = add(partials[: 2 * slots], swap(partials[2 * slots :], "tile"))
    else:
        pieces = lax.all_to_all(
            partials.reshape(tiles, 2 * slots, width), "tile", 0, 0, tiled=True
        )
        both = jnp.sum(pieces.astype(F32), axis=0).astype(BF16)
    summed = dict(zip(order, lax.optimization_barrier(cut(both))))
    results = {}
    for group in [[s] for s in steps[:-1]] + [[steps[-1], 0]]:
        back = cut(swap(join([summed[1, s] for s in group]), "expert"))
        for s, block in zip(group, back):
            total = add(summed[0, s], block)
            results[s] = trade(total, s) if s else total
    results = join([results[s] for s in range(experts)])
    return pl.pallas_call(
        combine_kernel,
        out_shape=jax.ShapeDtypeStruct((rows, width), BF16),
        in_specs=[vmem, vmem],
        out_specs=vmem,
        compiler_params=pltpu.CompilerParams(vmem_limit_bytes=4 * MIB),
        name="combine",
    )(comb, results)


def solution(mesh):
    placed = (
        P(("parts", "expert", "tile"), None),
        P(("parts", "expert", "tile"), None),
        P(("parts", "expert", "tile"), None),
        P("expert", None, "tile"),
        P("expert", None, "tile"),
        P("expert", "tile", None),
    )
    return jax.shard_map(
        shards,
        mesh=mesh,
        in_specs=placed,
        out_specs=P(("parts", "expert", "tile"), None),
        check_vma=False,
    )
```

```python
import functools

import jax
import jax.numpy as jnp
from jax import lax
from jax.experimental import pallas as pl
from jax.experimental.pallas import tpu as pltpu
from jax.sharding import PartitionSpec as P

F32 = jnp.float32
BF16 = jnp.bfloat16
MIB = 2**20


def partner(expert, step):
    return expert ^ step


def choose(steps, capacity, routes):
    me = lax.axis_index("expert") // 2
    slots, rows = len(steps) * capacity, routes.shape[1]
    slot = lax.broadcasted_iota(jnp.int32, (slots, rows), 0)
    block = slot // capacity
    place = slot - block * capacity
    expert = jnp.zeros_like(slot)
    for at, step in enumerate(steps):
        expert = jnp.where(block == at, partner(me, step), expert)
    first, second = routes[0:1, :] == expert, routes[1:2, :] == expert
    named = jnp.where(first | second, 1.0, 0.0)
    before = jnp.where(
        lax.broadcasted_iota(jnp.int32, (rows, rows), 0)
        < lax.broadcasted_iota(jnp.int32, (rows, rows), 1),
        1.0,
        0.0,
    )
    ahead = jnp.dot(named.astype(BF16), before.astype(BF16), preferred_element_type=F32)
    return jnp.where(ahead == place.astype(F32), named, 0.0), first


def route_kernel(steps, capacity, routes_hbm, tokens_hbm, out_ref, routes_ref, tokens_ref, sems):
    copies = [
        pltpu.make_async_copy(routes_hbm, routes_ref, sems.at[0]),
        pltpu.make_async_copy(tokens_hbm, tokens_ref, sems.at[1]),
    ]
    for copy in copies:
        copy.start()
    for copy in copies:
        copy.wait()
    chosen, _ = choose(steps, capacity, routes_ref[...])
    out_ref[...] = jnp.dot(
        chosen.astype(BF16), tokens_ref[...], preferred_element_type=F32
    ).astype(BF16)


def weigh_kernel(steps, capacity, routes_ref, weights_ref, comb_ref):
    chosen, first = choose(steps, capacity, routes_ref[...])
    weights = weights_ref[...].astype(F32)
    weight = jnp.where(first, weights[0:1, :], weights[1:2, :])
    comb_ref[...] = (chosen * weight).astype(BF16)


def ffn_kernel(width, rows_ref, gate_ref, up_ref, down_ref, out_ref, hidden_ref):
    for at in range(0, gate_ref.shape[1], width):
        part = slice(at, at + width)
        gate = jnp.dot(rows_ref[...], gate_ref[:, part], preferred_element_type=F32)
        up = jnp.dot(rows_ref[...], up_ref[:, part], preferred_element_type=F32)
        hidden_ref[:, part] = (gate / (1.0 + jnp.exp(-gate)) * up).astype(BF16)
    for at in range(0, down_ref.shape[1], 256):
        part = slice(at, at + 256)
        out_ref[:, part] = jnp.dot(
            hidden_ref[...], down_ref[:, part], preferred_element_type=F32
        ).astype(BF16)


def combine_kernel(comb_ref, results_ref, out_ref):
    out_ref[...] = lax.dot_general(
        comb_ref[...],
        results_ref[...],
        (((0,), (0,)), ((), ())),
        preferred_element_type=F32,
    ).astype(BF16)


def add(a, b):
    return (a.astype(F32) + b.astype(F32)).astype(BF16)


def shards(tokens, routes, route_weights, gate_proj, up_proj, down_proj):
    groups = lax.axis_size("expert")
    tiles = lax.axis_size("tile")
    experts = groups // 2
    rows, width = tokens.shape
    capacity = max(2, 2 * rows // experts)
    slots = experts * capacity
    steps = list(range(experts - 1, 0, -1))
    blocks = steps + [0]
    vmem = pl.BlockSpec(memory_space=pltpu.VMEM)
    hbm = pl.BlockSpec(memory_space=pltpu.HBM)
    small = pltpu.CompilerParams(vmem_limit_bytes=4 * MIB)
    outgoing = pl.pallas_call(
        functools.partial(route_kernel, blocks, capacity),
        out_shape=pltpu.VMEM((slots, width), BF16),
        in_specs=[hbm, hbm],
        out_specs=vmem,
        scratch_shapes=[
            pltpu.VMEM((2, rows), jnp.int32),
            pltpu.VMEM((rows, width), BF16),
            pltpu.SemaphoreType.DMA((2,)),
        ],
        cost_estimate=pl.CostEstimate(
            flops=10**12, bytes_accessed=4 * 10**8, transcendentals=0
        ),
        compiler_params=small,
        name="route",
    )(
        pltpu.with_memory_space_constraint(routes.T, pltpu.HBM),
        pltpu.with_memory_space_constraint(tokens, pltpu.HBM),
    )
    comb = pl.pallas_call(
        functools.partial(weigh_kernel, blocks, capacity),
        out_shape=jax.ShapeDtypeStruct((slots, rows), BF16),
        in_specs=[vmem, vmem],
        out_specs=vmem,
        compiler_params=small,
        name="weigh",
    )(routes.T, route_weights.T)

    def trade(x, step):
        pairs = [(g, 2 * partner(g // 2, step) + g % 2) for g in range(groups)]
        return lax.ppermute(x, "expert", pairs)

    def swap(x, axis):
        return lax.ppermute(x, axis, [(i, i ^ 1) for i in range(lax.axis_size(axis))])

    def join(blocks):
        return jnp.concatenate(blocks) if len(blocks) > 1 else blocks[0]

    def cut(block):
        return list(block.reshape(-1, capacity, width))

    sent = dict(zip(blocks, cut(outgoing)))
    here = {s: trade(sent[s], s) for s in steps}
    here[0] = sent[0]
    there = {}
    for group in [[0, steps[0]]] + [[s] for s in steps[1:]]:
        there.update(zip(group, cut(swap(join([here[s] for s in group]), "expert"))))
    order = [(side, s) for side in (0, 1) for s in [0] + steps]
    both = join([side[s] for side in (here, there) for s in [0] + steps])
    if tiles == 2:
        received = join([both, swap(both, "tile")])
    else:
        received = lax.all_gather(both, "tile", axis=0, tiled=True)
    gate, up, down = gate_proj[0], up_proj[0], down_proj[0]
    count, hidden = received.shape[0], gate.shape[1]
    block = min(512, hidden)
    partials = pl.pallas_call(
        functools.partial(ffn_kernel, block),
        out_shape=jax.ShapeDtypeStruct((count, width), BF16),
        in_specs=[vmem, vmem, vmem, vmem],
        out_specs=vmem,
        scratch_shapes=[
            pltpu.VMEM((count, hidden), BF16),
        ],
        compiler_params=pltpu.CompilerParams(vmem_limit_bytes=8 * MIB),
        cost_estimate=pl.CostEstimate(
            flops=6 * count * width * hidden,
            bytes_accessed=6 * width * hidden,
            transcendentals=count * hidden,
        ),
        name="ffn",
    )(received, gate, up, down)
    if tiles == 2:
        both = add(partials[: 2 * slots], swap(partials[2 * slots :], "tile"))
    else:
        pieces = lax.all_to_all(
            partials.reshape(tiles, 2 * slots, width), "tile", 0, 0, tiled=True
        )
        both = jnp.sum(pieces.astype(F32), axis=0).astype(BF16)
    summed = dict(zip(order, lax.optimization_barrier(cut(both))))
    results = {}
    for s in blocks:
        leaving = summed[1, s]
        if s == 0:
            leaving, _ = lax.optimization_barrier((leaving, back))
        back = swap(leaving, "expert")
        total = add(summed[0, s], back)
        results[s] = trade(total, s) if s else total
    results = join([results[s] for s in blocks])
    return pl.pallas_call(
        combine_kernel,
        out_shape=jax.ShapeDtypeStruct((rows, width), BF16),
        in_specs=[vmem, vmem],
        out_specs=vmem,
        compiler_params=pltpu.CompilerParams(vmem_limit_bytes=4 * MIB),
        name="combine",
    )(comb, results)


def solution(mesh):
    placed = (
        P(("parts", "expert", "tile"), None),
        P(("parts", "expert", "tile"), None),
        P(("parts", "expert", "tile"), None),
        P("expert", None, "tile"),
        P("expert", None, "tile"),
        P("expert", "tile", None),
    )
    return jax.shard_map(
        shards,
        mesh=mesh,
        in_specs=placed,
        out_specs=P(("parts", "expert", "tile"), None),
        check_vma=False,
    )
```

```python
import functools

import jax
import jax.numpy as jnp
from jax import lax
from jax.experimental import pallas as pl
from jax.experimental.pallas import tpu as pltpu
from jax.sharding import PartitionSpec as P

F32 = jnp.float32
BF16 = jnp.bfloat16
MIB = 2**20


def partner(expert, step):
    return expert ^ step


def choose(steps, capacity, routes):
    me = lax.axis_index("expert") // 2
    slots, rows = len(steps) * capacity, routes.shape[1]
    slot = lax.broadcasted_iota(jnp.int32, (slots, rows), 0)
    block = slot // capacity
    place = slot - block * capacity
    expert = jnp.zeros_like(slot)
    for at, step in enumerate(steps):
        expert = jnp.where(block == at, partner(me, step), expert)
    first, second = routes[0:1, :] == expert, routes[1:2, :] == expert
    named = jnp.where(first | second, 1.0, 0.0)
    before = jnp.where(
        lax.broadcasted_iota(jnp.int32, (rows, rows), 0)
        < lax.broadcasted_iota(jnp.int32, (rows, rows), 1),
        1.0,
        0.0,
    )
    ahead = jnp.dot(named.astype(BF16), before.astype(BF16), preferred_element_type=F32)
    return jnp.where(ahead == place.astype(F32), named, 0.0), first


def route_kernel(steps, capacity, routes_hbm, tokens_hbm, out_ref, routes_ref, tokens_ref, sems):
    copies = [
        pltpu.make_async_copy(routes_hbm, routes_ref, sems.at[0]),
        pltpu.make_async_copy(tokens_hbm, tokens_ref, sems.at[1]),
    ]
    for copy in copies:
        copy.start()
    for copy in copies:
        copy.wait()
    chosen, _ = choose(steps, capacity, routes_ref[...])
    out_ref[...] = jnp.dot(
        chosen.astype(BF16), tokens_ref[...], preferred_element_type=F32
    ).astype(BF16)


def weigh_kernel(steps, capacity, routes_ref, weights_ref, comb_ref):
    chosen, first = choose(steps, capacity, routes_ref[...])
    weights = weights_ref[...].astype(F32)
    weight = jnp.where(first, weights[0:1, :], weights[1:2, :])
    comb_ref[...] = (chosen * weight).astype(BF16)


def ffn_kernel(width, rows_ref, gate_ref, up_ref, down_ref, out_ref, hidden_ref):
    for at in range(0, gate_ref.shape[1], width):
        part = slice(at, at + width)
        gate = jnp.dot(rows_ref[...], gate_ref[:, part], preferred_element_type=F32)
        up = jnp.dot(rows_ref[...], up_ref[:, part], preferred_element_type=F32)
        hidden_ref[:, part] = (gate / (1.0 + jnp.exp(-gate)) * up).astype(BF16)
    for at in range(0, down_ref.shape[1], 256):
        part = slice(at, at + 256)
        out_ref[:, part] = jnp.dot(
            hidden_ref[...], down_ref[:, part], preferred_element_type=F32
        ).astype(BF16)


def combine_kernel(comb_ref, results_ref, out_ref):
    out_ref[...] = lax.dot_general(
        comb_ref[...],
        results_ref[...],
        (((0,), (0,)), ((), ())),
        preferred_element_type=F32,
    ).astype(BF16)


def add(a, b):
    return (a.astype(F32) + b.astype(F32)).astype(BF16)


def shards(tokens, routes, route_weights, gate_proj, up_proj, down_proj):
    groups = lax.axis_size("expert")
    tiles = lax.axis_size("tile")
    experts = groups // 2
    rows, width = tokens.shape
    capacity = max(2, 2 * rows // experts)
    slots = experts * capacity
    steps = list(range(experts - 1, 0, -1))
    blocks = steps + [0]
    vmem = pl.BlockSpec(memory_space=pltpu.VMEM)
    hbm = pl.BlockSpec(memory_space=pltpu.HBM)
    small = pltpu.CompilerParams(vmem_limit_bytes=4 * MIB)
    outgoing = pl.pallas_call(
        functools.partial(route_kernel, blocks, capacity),
        out_shape=pltpu.VMEM((slots, width), BF16),
        in_specs=[hbm, hbm],
        out_specs=vmem,
        scratch_shapes=[
            pltpu.VMEM((2, rows), jnp.int32),
            pltpu.VMEM((rows, width), BF16),
            pltpu.SemaphoreType.DMA((2,)),
        ],
        cost_estimate=pl.CostEstimate(
            flops=10**12, bytes_accessed=4 * 10**8, transcendentals=0
        ),
        compiler_params=small,
        name="route",
    )(
        pltpu.with_memory_space_constraint(routes.T, pltpu.HBM),
        pltpu.with_memory_space_constraint(tokens, pltpu.HBM),
    )
    comb = pl.pallas_call(
        functools.partial(weigh_kernel, blocks, capacity),
        out_shape=jax.ShapeDtypeStruct((slots, rows), BF16),
        in_specs=[vmem, vmem],
        out_specs=vmem,
        compiler_params=small,
        name="weigh",
    )(routes.T, route_weights.T)

    def trade(x, step):
        pairs = [(g, 2 * partner(g // 2, step) + g % 2) for g in range(groups)]
        return lax.ppermute(x, "expert", pairs)

    def swap(x, axis):
        return lax.ppermute(x, axis, [(i, i ^ 1) for i in range(lax.axis_size(axis))])

    def join(blocks):
        return jnp.concatenate(blocks) if len(blocks) > 1 else blocks[0]

    def cut(block):
        return list(block.reshape(-1, capacity, width))

    sent = dict(zip(blocks, cut(outgoing)))
    here = {s: trade(sent[s], s) for s in steps}
    here[0] = sent[0]
    there = {}
    for group in [[0]] + [[s] for s in steps]:
        there.update(zip(group, cut(swap(join([here[s] for s in group]), "expert"))))
    order = [(side, s) for side in (0, 1) for s in [0] + steps]
    names = [(side, s) for side in (here, there) for s in [0] + steps]
    pieces = [join([side[s] for side, s in names[:-2]]), join([side[s] for side, s in names[-2:]])]
    both = join(pieces)
    if tiles == 2:
        received = join(pieces + [swap(piece, "tile") for piece in pieces])
    else:
        received = lax.all_gather(both, "tile", axis=0, tiled=True)
    gate, up, down = gate_proj[0], up_proj[0], down_proj[0]
    count, hidden = received.shape[0], gate.shape[1]
    block = min(512, hidden)
    partials = pl.pallas_call(
        functools.partial(ffn_kernel, block),
        out_shape=jax.ShapeDtypeStruct((count, width), BF16),
        in_specs=[vmem, vmem, vmem, vmem],
        out_specs=vmem,
        scratch_shapes=[
            pltpu.VMEM((count, hidden), BF16),
        ],
        compiler_params=pltpu.CompilerParams(vmem_limit_bytes=8 * MIB),
        cost_estimate=pl.CostEstimate(
            flops=6 * count * width * hidden,
            bytes_accessed=6 * width * hidden,
            transcendentals=count * hidden,
        ),
        name="ffn",
    )(received, gate, up, down)
    if tiles == 2:
        kept, left = [dict(zip(order, cut(rows))) for rows in jnp.split(partials, 2)]
        summed = {}
        for group in (steps[:-1], [steps[-1], 0]):
            moved = [key for key in order if key[1] in group]
            both = add(join([kept[key] for key in moved]), swap(join([left[key] for key in moved]), "tile"))
            summed.update(zip(moved, lax.optimization_barrier(cut(both))))
    else:
        pieces = lax.all_to_all(
            partials.reshape(tiles, 2 * slots, width), "tile", 0, 0, tiled=True
        )
        both = jnp.sum(pieces.astype(F32), axis=0).astype(BF16)
        summed = dict(zip(order, lax.optimization_barrier(cut(both))))
    results = {}
    for s in blocks:
        leaving = summed[1, s]
        if s == 0:
            leaving, _ = lax.optimization_barrier((leaving, back))
        back = swap(leaving, "expert")
        total = add(summed[0, s], back)
        results[s] = trade(total, s) if s else total
    results = join([results[s] for s in blocks])
    return pl.pallas_call(
        combine_kernel,
        out_shape=jax.ShapeDtypeStruct((rows, width), BF16),
        in_specs=[vmem, vmem],
        out_specs=vmem,
        compiler_params=pltpu.CompilerParams(vmem_limit_bytes=4 * MIB),
        name="combine",
    )(comb, results)


def solution(mesh):
    placed = (
        P(("parts", "expert", "tile"), None),
        P(("parts", "expert", "tile"), None),
        P(("parts", "expert", "tile"), None),
        P("expert", None, "tile"),
        P("expert", None, "tile"),
        P("expert", "tile", None),
    )
    return jax.shard_map(
        shards,
        mesh=mesh,
        in_specs=placed,
        out_specs=P(("parts", "expert", "tile"), None),
        check_vma=False,
    )
```

```python
import functools

import jax
import jax.numpy as jnp
from jax import lax
from jax.experimental import pallas as pl
from jax.experimental.pallas import tpu as pltpu
from jax.sharding import PartitionSpec as P

F32 = jnp.float32
BF16 = jnp.bfloat16
MIB = 2**20


def partner(expert, step):
    return expert ^ step


def choose(steps, capacity, routes):
    me = lax.axis_index("expert") // 2
    slots, rows = len(steps) * capacity, routes.shape[1]
    slot = lax.broadcasted_iota(jnp.int32, (slots, rows), 0)
    block = slot // capacity
    place = slot - block * capacity
    expert = jnp.zeros_like(slot)
    for at, step in enumerate(steps):
        expert = jnp.where(block == at, partner(me, step), expert)
    first, second = routes[0:1, :] == expert, routes[1:2, :] == expert
    named = jnp.where(first | second, 1.0, 0.0)
    before = jnp.where(
        lax.broadcasted_iota(jnp.int32, (rows, rows), 0)
        < lax.broadcasted_iota(jnp.int32, (rows, rows), 1),
        1.0,
        0.0,
    )
    ahead = jnp.dot(named.astype(BF16), before.astype(BF16), preferred_element_type=F32)
    return jnp.where(ahead == place.astype(F32), named, 0.0), first


def route_kernel(steps, capacity, routes_hbm, tokens_hbm, out_ref, routes_ref, tokens_ref, sems):
    copies = [
        pltpu.make_async_copy(routes_hbm, routes_ref, sems.at[0]),
        pltpu.make_async_copy(tokens_hbm, tokens_ref, sems.at[1]),
    ]
    for copy in copies:
        copy.start()
    copies[0].wait()
    chosen, _ = choose(steps, capacity, routes_ref[...])
    copies[1].wait()
    out_ref[...] = jnp.dot(
        chosen.astype(BF16), tokens_ref[...], preferred_element_type=F32
    ).astype(BF16)


def weigh_kernel(steps, capacity, routes_ref, weights_ref, comb_ref):
    chosen, first = choose(steps, capacity, routes_ref[...])
    weights = weights_ref[...].astype(F32)
    weight = jnp.where(first, weights[0:1, :], weights[1:2, :])
    comb_ref[...] = (chosen * weight).astype(BF16)


def ffn_kernel(width, rows_ref, gate_ref, up_ref, down_ref, out_ref, hidden_ref):
    for at in range(0, gate_ref.shape[1], width):
        part = slice(at, at + width)
        gate = jnp.dot(rows_ref[...], gate_ref[:, part], preferred_element_type=F32)
        up = jnp.dot(rows_ref[...], up_ref[:, part], preferred_element_type=F32)
        hidden_ref[:, part] = (gate / (1.0 + jnp.exp(-gate)) * up).astype(BF16)
    for at in range(0, down_ref.shape[1], 256):
        part = slice(at, at + 256)
        out_ref[:, part] = jnp.dot(
            hidden_ref[...], down_ref[:, part], preferred_element_type=F32
        ).astype(BF16)


def combine_kernel(comb_ref, results_ref, out_ref):
    out_ref[...] = lax.dot_general(
        comb_ref[...],
        results_ref[...],
        (((0,), (0,)), ((), ())),
        preferred_element_type=F32,
    ).astype(BF16)


def add(a, b):
    return (a.astype(F32) + b.astype(F32)).astype(BF16)


def shards(tokens, routes, route_weights, gate_proj, up_proj, down_proj):
    groups = lax.axis_size("expert")
    tiles = lax.axis_size("tile")
    experts = groups // 2
    rows, width = tokens.shape
    capacity = max(2, 2 * rows // experts)
    slots = experts * capacity
    steps = list(range(experts - 1, 0, -1))
    blocks = steps + [0]
    vmem = pl.BlockSpec(memory_space=pltpu.VMEM)
    hbm = pl.BlockSpec(memory_space=pltpu.HBM)
    small = pltpu.CompilerParams(vmem_limit_bytes=4 * MIB)
    outgoing = pl.pallas_call(
        functools.partial(route_kernel, blocks, capacity),
        out_shape=pltpu.VMEM((slots, width), BF16),
        in_specs=[hbm, hbm],
        out_specs=vmem,
        scratch_shapes=[
            pltpu.VMEM((2, rows), jnp.int32),
            pltpu.VMEM((rows, width), BF16),
            pltpu.SemaphoreType.DMA((2,)),
        ],
        cost_estimate=pl.CostEstimate(
            flops=10**12, bytes_accessed=4 * 10**8, transcendentals=0
        ),
        compiler_params=small,
        name="route",
    )(
        pltpu.with_memory_space_constraint(routes.T, pltpu.HBM),
        pltpu.with_memory_space_constraint(tokens, pltpu.HBM),
    )
    comb = pl.pallas_call(
        functools.partial(weigh_kernel, blocks, capacity),
        out_shape=jax.ShapeDtypeStruct((slots, rows), BF16),
        in_specs=[vmem, vmem],
        out_specs=vmem,
        compiler_params=small,
        name="weigh",
    )(routes.T, route_weights.T)

    def trade(x, step):
        pairs = [(g, 2 * partner(g // 2, step) + g % 2) for g in range(groups)]
        return lax.ppermute(x, "expert", pairs)

    def swap(x, axis):
        return lax.ppermute(x, axis, [(i, i ^ 1) for i in range(lax.axis_size(axis))])

    def join(blocks):
        return jnp.concatenate(blocks) if len(blocks) > 1 else blocks[0]

    def cut(block):
        return list(block.reshape(-1, capacity, width))

    sent = dict(zip(blocks, cut(outgoing)))
    here = {s: trade(sent[s], s) for s in steps}
    here[0] = sent[0]
    there = {}
    for group in [[0]] + [[s] for s in steps]:
        there.update(zip(group, cut(swap(join([here[s] for s in group]), "expert"))))
    order = [(side, s) for side in (0, 1) for s in [0] + steps]
    names = [(side, s) for side in (here, there) for s in [0] + steps]
    pieces = [join([side[s] for side, s in names[:-1]]), join([side[s] for side, s in names[-1:]])]
    both = join(pieces)
    if tiles == 2:
        received = join(pieces + [swap(piece, "tile") for piece in pieces])
    else:
        received = lax.all_gather(both, "tile", axis=0, tiled=True)
    gate, up, down = gate_proj[0], up_proj[0], down_proj[0]
    count, hidden = received.shape[0], gate.shape[1]
    block = min(512, hidden)
    partials = pl.pallas_call(
        functools.partial(ffn_kernel, block),
        out_shape=jax.ShapeDtypeStruct((count, width), BF16),
        in_specs=[vmem, vmem, vmem, vmem],
        out_specs=vmem,
        scratch_shapes=[
            pltpu.VMEM((count, hidden), BF16),
        ],
        compiler_params=pltpu.CompilerParams(vmem_limit_bytes=8 * MIB),
        cost_estimate=pl.CostEstimate(
            flops=6 * count * width * hidden,
            bytes_accessed=6 * width * hidden,
            transcendentals=count * hidden,
        ),
        name="ffn",
    )(received, gate, up, down)
    if tiles == 2:
        kept, left = [dict(zip(order, cut(rows))) for rows in jnp.split(partials, 2)]
        summed = {}
        for group in (steps[:-1], [steps[-1], 0]):
            moved = [key for key in order if key[1] in group]
            both = add(join([kept[key] for key in moved]), swap(join([left[key] for key in moved]), "tile"))
            summed.update(zip(moved, lax.optimization_barrier(cut(both))))
    else:
        pieces = lax.all_to_all(
            partials.reshape(tiles, 2 * slots, width), "tile", 0, 0, tiled=True
        )
        both = jnp.sum(pieces.astype(F32), axis=0).astype(BF16)
        summed = dict(zip(order, lax.optimization_barrier(cut(both))))
    results = {}
    for group in [[s] for s in steps[:-1]] + [[steps[-1], 0]]:
        back = swap(join([summed[1, s] for s in group]), "expert")
        for s, block in zip(group, cut(back)):
            total = add(summed[0, s], block)
            results[s] = trade(total, s) if s else total
    results = join([results[s] for s in blocks])
    return pl.pallas_call(
        combine_kernel,
        out_shape=jax.ShapeDtypeStruct((rows, width), BF16),
        in_specs=[vmem, vmem],
        out_specs=vmem,
        compiler_params=pltpu.CompilerParams(vmem_limit_bytes=4 * MIB),
        name="combine",
    )(comb, results)


def solution(mesh):
    placed = (
        P(("parts", "expert", "tile"), None),
        P(("parts", "expert", "tile"), None),
        P(("parts", "expert", "tile"), None),
        P("expert", None, "tile"),
        P("expert", None, "tile"),
        P("expert", "tile", None),
    )
    return jax.shard_map(
        shards,
        mesh=mesh,
        in_specs=placed,
        out_specs=P(("parts", "expert", "tile"), None),
        check_vma=False,
    )
```

```python
import functools

import jax
import jax.numpy as jnp
from jax import lax
from jax.experimental import pallas as pl
from jax.experimental.pallas import tpu as pltpu
from jax.sharding import PartitionSpec as P

F32 = jnp.float32
BF16 = jnp.bfloat16
MIB = 2**20


def partner(expert, step):
    return expert ^ step


def choose(steps, capacity, routes):
    me = lax.axis_index("expert") // 2
    slots, rows = len(steps) * capacity, routes.shape[1]
    slot = lax.broadcasted_iota(jnp.int32, (slots, rows), 0)
    block = slot // capacity
    place = slot - block * capacity
    expert = jnp.zeros_like(slot)
    for at, step in enumerate(steps):
        expert = jnp.where(block == at, partner(me, step), expert)
    first, second = routes[0:1, :] == expert, routes[1:2, :] == expert
    named = jnp.where(first | second, 1.0, 0.0)
    before = jnp.where(
        lax.broadcasted_iota(jnp.int32, (rows, rows), 0)
        < lax.broadcasted_iota(jnp.int32, (rows, rows), 1),
        1.0,
        0.0,
    )
    ahead = jnp.dot(named.astype(BF16), before.astype(BF16), preferred_element_type=F32)
    return jnp.where(ahead == place.astype(F32), named, 0.0), first


def route_kernel(steps, capacity, routes_hbm, tokens_hbm, out_ref, routes_ref, tokens_ref, sems):
    copies = [
        pltpu.make_async_copy(routes_hbm, routes_ref, sems.at[0]),
        pltpu.make_async_copy(tokens_hbm, tokens_ref, sems.at[1]),
    ]
    for copy in copies:
        copy.start()
    copies[0].wait()
    chosen, _ = choose(steps, capacity, routes_ref[...])
    copies[1].wait()
    out_ref[...] = jnp.dot(
        chosen.astype(BF16), tokens_ref[...], preferred_element_type=F32
    ).astype(BF16)


def weigh_kernel(steps, capacity, routes_ref, weights_ref, comb_ref):
    chosen, first = choose(steps, capacity, routes_ref[...])
    weights = weights_ref[...].astype(F32)
    weight = jnp.where(first, weights[0:1, :], weights[1:2, :])
    comb_ref[...] = (chosen * weight).astype(BF16)


def ffn_kernel(width, rows_ref, gate_ref, up_ref, down_ref, out_ref, hidden_ref):
    for at in range(0, gate_ref.shape[1], width):
        part = slice(at, at + width)
        gate = jnp.dot(rows_ref[...], gate_ref[:, part], preferred_element_type=F32)
        up = jnp.dot(rows_ref[...], up_ref[:, part], preferred_element_type=F32)
        hidden_ref[:, part] = (gate / (1.0 + jnp.exp(-gate)) * up).astype(BF16)
    for at in range(0, down_ref.shape[1], 256):
        part = slice(at, at + 256)
        out_ref[:, part] = jnp.dot(
            hidden_ref[...], down_ref[:, part], preferred_element_type=F32
        ).astype(BF16)


def combine_kernel(comb_ref, results_ref, out_ref):
    out_ref[...] = lax.dot_general(
        comb_ref[...],
        results_ref[...],
        (((0,), (0,)), ((), ())),
        preferred_element_type=F32,
    ).astype(BF16)


def add(a, b):
    return (a.astype(F32) + b.astype(F32)).astype(BF16)


def shards(tokens, routes, route_weights, gate_proj, up_proj, down_proj):
    groups = lax.axis_size("expert")
    tiles = lax.axis_size("tile")
    experts = groups // 2
    rows, width = tokens.shape
    capacity = max(2, 2 * rows // experts)
    slots = experts * capacity
    steps = list(range(experts - 1, 0, -1))
    blocks = steps + [0]
    vmem = pl.BlockSpec(memory_space=pltpu.VMEM)
    hbm = pl.BlockSpec(memory_space=pltpu.HBM)
    small = pltpu.CompilerParams(vmem_limit_bytes=4 * MIB)
    outgoing = pl.pallas_call(
        functools.partial(route_kernel, blocks, capacity),
        out_shape=pltpu.VMEM((slots, width), BF16),
        in_specs=[hbm, hbm],
        out_specs=vmem,
        scratch_shapes=[
            pltpu.VMEM((2, rows), jnp.int32),
            pltpu.VMEM((rows, width), BF16),
            pltpu.SemaphoreType.DMA((2,)),
        ],
        cost_estimate=pl.CostEstimate(
            flops=10**12, bytes_accessed=4 * 10**8, transcendentals=0
        ),
        compiler_params=small,
        name="route",
    )(
        pltpu.with_memory_space_constraint(routes.T, pltpu.HBM),
        pltpu.with_memory_space_constraint(tokens, pltpu.HBM),
    )
    comb = pl.pallas_call(
        functools.partial(weigh_kernel, blocks, capacity),
        out_shape=jax.ShapeDtypeStruct((slots, rows), BF16),
        in_specs=[vmem, vmem],
        out_specs=vmem,
        compiler_params=small,
        name="weigh",
    )(routes.T, route_weights.T)

    def trade(x, step):
        pairs = [(g, 2 * partner(g // 2, step) + g % 2) for g in range(groups)]
        return lax.ppermute(x, "expert", pairs)

    def swap(x, axis):
        return lax.ppermute(x, axis, [(i, i ^ 1) for i in range(lax.axis_size(axis))])

    def join(blocks):
        return jnp.concatenate(blocks) if len(blocks) > 1 else blocks[0]

    def cut(block):
        return list(block.reshape(-1, capacity, width))

    sent = dict(zip(blocks, cut(outgoing)))
    here = {s: trade(sent[s], s) for s in steps}
    here[0] = sent[0]
    arrival = [0, steps[-1]] + steps[:-1]
    there = {}
    for s in arrival:
        there[s] = swap(here[s], "expert")
    order = [(side, s) for side in (0, 1) for s in arrival]
    names = [(side, s) for side in (here, there) for s in arrival]
    pieces = [join([side[s] for side, s in names[:-1]]), join([side[s] for side, s in names[-1:]])]
    both = join(pieces)
    if tiles == 2:
        received = join(pieces + [swap(piece, "tile") for piece in pieces])
    else:
        received = lax.all_gather(both, "tile", axis=0, tiled=True)
    gate, up, down = gate_proj[0], up_proj[0], down_proj[0]
    count, hidden = received.shape[0], gate.shape[1]
    block = min(512, hidden)
    partials = pl.pallas_call(
        functools.partial(ffn_kernel, block),
        out_shape=jax.ShapeDtypeStruct((count, width), BF16),
        in_specs=[vmem, vmem, vmem, vmem],
        out_specs=vmem,
        scratch_shapes=[
            pltpu.VMEM((count, hidden), BF16),
        ],
        compiler_params=pltpu.CompilerParams(vmem_limit_bytes=8 * MIB),
        cost_estimate=pl.CostEstimate(
            flops=6 * count * width * hidden,
            bytes_accessed=6 * width * hidden,
            transcendentals=count * hidden,
        ),
        name="ffn",
    )(received, gate, up, down)
    if tiles == 2:
        kept, left = [dict(zip(order, cut(rows))) for rows in jnp.split(partials, 2)]
        summed = {}
        for group in (steps[:-1], [steps[-1], 0]):
            moved = [key for key in order if key[1] in group]
            both = add(join([kept[key] for key in moved]), swap(join([left[key] for key in moved]), "tile"))
            summed.update(zip(moved, lax.optimization_barrier(cut(both))))
    else:
        pieces = lax.all_to_all(
            partials.reshape(tiles, 2 * slots, width), "tile", 0, 0, tiled=True
        )
        both = jnp.sum(pieces.astype(F32), axis=0).astype(BF16)
        summed = dict(zip(order, lax.optimization_barrier(cut(both))))
    results = {}
    for group in [[s] for s in steps[:-1]] + [[steps[-1], 0]]:
        back = swap(join([summed[1, s] for s in group]), "expert")
        for s, block in zip(group, cut(back)):
            total = add(summed[0, s], block)
            results[s] = trade(total, s) if s else total
    results = join([results[s] for s in blocks])
    return pl.pallas_call(
        combine_kernel,
        out_shape=jax.ShapeDtypeStruct((rows, width), BF16),
        in_specs=[vmem, vmem],
        out_specs=vmem,
        compiler_params=pltpu.CompilerParams(vmem_limit_bytes=4 * MIB),
        name="combine",
    )(comb, results)


def solution(mesh):
    placed = (
        P(("parts", "expert", "tile"), None),
        P(("parts", "expert", "tile"), None),
        P(("parts", "expert", "tile"), None),
        P("expert", None, "tile"),
        P("expert", None, "tile"),
        P("expert", "tile", None),
    )
    return jax.shard_map(
        shards,
        mesh=mesh,
        in_specs=placed,
        out_specs=P(("parts", "expert", "tile"), None),
        check_vma=False,
    )
```

```python
import functools

import jax
import jax.numpy as jnp
from jax import lax
from jax.experimental import pallas as pl
from jax.experimental.pallas import tpu as pltpu
from jax.sharding import PartitionSpec as P

F32 = jnp.float32
BF16 = jnp.bfloat16
MIB = 2**20


def partner(expert, step):
    return expert ^ step


def choose(steps, capacity, routes):
    me = lax.axis_index("expert") // 2
    slots, rows = len(steps) * capacity, routes.shape[1]
    slot = lax.broadcasted_iota(jnp.int32, (slots, rows), 0)
    block = slot // capacity
    place = slot - block * capacity
    expert = jnp.zeros_like(slot)
    for at, step in enumerate(steps):
        expert = jnp.where(block == at, partner(me, step), expert)
    first, second = routes[0:1, :] == expert, routes[1:2, :] == expert
    named = jnp.where(first | second, 1.0, 0.0)
    before = jnp.where(
        lax.broadcasted_iota(jnp.int32, (rows, rows), 0)
        < lax.broadcasted_iota(jnp.int32, (rows, rows), 1),
        1.0,
        0.0,
    )
    ahead = jnp.dot(named.astype(BF16), before.astype(BF16), preferred_element_type=F32)
    return jnp.where(ahead == place.astype(F32), named, 0.0), first


def route_kernel(steps, capacity, routes_hbm, tokens_hbm, out_ref, routes_ref, tokens_ref, sems):
    copies = [
        pltpu.make_async_copy(routes_hbm, routes_ref, sems.at[0]),
        pltpu.make_async_copy(tokens_hbm, tokens_ref, sems.at[1]),
    ]
    for copy in copies:
        copy.start()
    copies[0].wait()
    chosen, _ = choose(steps, capacity, routes_ref[...])
    copies[1].wait()
    out_ref[...] = jnp.dot(
        chosen.astype(BF16), tokens_ref[...], preferred_element_type=F32
    ).astype(BF16)


def weigh_kernel(steps, capacity, routes_ref, weights_ref, comb_ref):
    chosen, first = choose(steps, capacity, routes_ref[...])
    weights = weights_ref[...].astype(F32)
    weight = jnp.where(first, weights[0:1, :], weights[1:2, :])
    comb_ref[...] = (chosen * weight).astype(BF16)


def ffn_kernel(width, rows_ref, gate_ref, up_ref, down_ref, out_ref, hidden_ref):
    for at in range(0, gate_ref.shape[1], width):
        part = slice(at, at + width)
        gate = jnp.dot(rows_ref[...], gate_ref[:, part], preferred_element_type=F32)
        up = jnp.dot(rows_ref[...], up_ref[:, part], preferred_element_type=F32)
        hidden_ref[:, part] = (gate / (1.0 + jnp.exp(-gate)) * up).astype(BF16)
    for at in range(0, down_ref.shape[1], 256):
        part = slice(at, at + 256)
        out_ref[:, part] = jnp.dot(
            hidden_ref[...], down_ref[:, part], preferred_element_type=F32
        ).astype(BF16)


def combine_kernel(comb_ref, results_ref, out_ref):
    out_ref[...] = lax.dot_general(
        comb_ref[...],
        results_ref[...],
        (((0,), (0,)), ((), ())),
        preferred_element_type=F32,
    ).astype(BF16)


def add(a, b):
    return (a.astype(F32) + b.astype(F32)).astype(BF16)


def shards(tokens, routes, route_weights, gate_proj, up_proj, down_proj):
    groups = lax.axis_size("expert")
    tiles = lax.axis_size("tile")
    experts = groups // 2
    rows, width = tokens.shape
    capacity = max(2, 2 * rows // experts)
    slots = experts * capacity
    steps = list(range(experts - 1, 0, -1))
    blocks = steps + [0]
    vmem = pl.BlockSpec(memory_space=pltpu.VMEM)
    hbm = pl.BlockSpec(memory_space=pltpu.HBM)
    small = pltpu.CompilerParams(vmem_limit_bytes=4 * MIB)
    outgoing = pl.pallas_call(
        functools.partial(route_kernel, blocks, capacity),
        out_shape=pltpu.VMEM((slots, width), BF16),
        in_specs=[hbm, hbm],
        out_specs=vmem,
        scratch_shapes=[
            pltpu.VMEM((2, rows), jnp.int32),
            pltpu.VMEM((rows, width), BF16),
            pltpu.SemaphoreType.DMA((2,)),
        ],
        cost_estimate=pl.CostEstimate(
            flops=10**12, bytes_accessed=4 * 10**8, transcendentals=0
        ),
        compiler_params=small,
        name="route",
    )(
        pltpu.with_memory_space_constraint(routes.T, pltpu.HBM),
        pltpu.with_memory_space_constraint(tokens, pltpu.HBM),
    )
    comb = pl.pallas_call(
        functools.partial(weigh_kernel, blocks, capacity),
        out_shape=jax.ShapeDtypeStruct((slots, rows), BF16),
        in_specs=[vmem, vmem],
        out_specs=vmem,
        compiler_params=small,
        name="weigh",
    )(routes.T, route_weights.T)

    def trade(x, step):
        pairs = [(g, 2 * partner(g // 2, step) + g % 2) for g in range(groups)]
        return lax.ppermute(x, "expert", pairs)

    def swap(x, axis):
        return lax.ppermute(x, axis, [(i, i ^ 1) for i in range(lax.axis_size(axis))])

    def join(blocks):
        return jnp.concatenate(blocks) if len(blocks) > 1 else blocks[0]

    def cut(block):
        return list(block.reshape(-1, capacity, width))

    sent = dict(zip(blocks, cut(outgoing)))
    here = {s: trade(sent[s], s) for s in steps}
    here[0] = sent[0]
    arrival = [0, steps[-1]] + steps[:-1]
    there = {}
    for s in arrival:
        there[s] = swap(here[s], "expert")
    order = [(side, s) for side in (0, 1) for s in arrival]
    names = [(side, s) for side in (here, there) for s in arrival]
    pieces = [join([side[s] for side, s in names[:-1]]), join([side[s] for side, s in names[-1:]])]
    both = join(pieces)
    if tiles == 2:
        received = join(pieces + [swap(piece, "tile") for piece in pieces])
    else:
        received = lax.all_gather(both, "tile", axis=0, tiled=True)
    gate, up, down = gate_proj[0], up_proj[0], down_proj[0]
    count, hidden = received.shape[0], gate.shape[1]
    block = min(512, hidden)
    partials = pl.pallas_call(
        functools.partial(ffn_kernel, block),
        out_shape=jax.ShapeDtypeStruct((count, width), BF16),
        in_specs=[vmem, vmem, vmem, vmem],
        out_specs=vmem,
        scratch_shapes=[
            pltpu.VMEM((count, hidden), BF16),
        ],
        compiler_params=pltpu.CompilerParams(vmem_limit_bytes=8 * MIB),
        cost_estimate=pl.CostEstimate(
            flops=6 * count * width * hidden,
            bytes_accessed=6 * width * hidden,
            transcendentals=count * hidden,
        ),
        name="ffn",
    )(received, gate, up, down)
    if tiles == 2:
        kept, left = [dict(zip(order, cut(rows))) for rows in jnp.split(partials, 2)]
        summed = {}
        for group in (steps[:-1], [steps[-1], 0]):
            moved = [key for key in order if key[1] in group]
            both = add(join([kept[key] for key in moved]), swap(join([left[key] for key in moved]), "tile"))
            summed.update(zip(moved, lax.optimization_barrier(cut(both))))
    else:
        pieces = lax.all_to_all(
            partials.reshape(tiles, 2 * slots, width), "tile", 0, 0, tiled=True
        )
        both = jnp.sum(pieces.astype(F32), axis=0).astype(BF16)
        summed = dict(zip(order, lax.optimization_barrier(cut(both))))
    results = {}
    for group in [[s] for s in blocks]:
        back = swap(join([summed[1, s] for s in group]), "expert")
        for s, block in zip(group, cut(back)):
            total = add(summed[0, s], block)
            results[s] = trade(total, s) if s else total
    results = join([results[s] for s in blocks])
    return pl.pallas_call(
        combine_kernel,
        out_shape=jax.ShapeDtypeStruct((rows, width), BF16),
        in_specs=[vmem, vmem],
        out_specs=vmem,
        compiler_params=pltpu.CompilerParams(vmem_limit_bytes=4 * MIB),
        name="combine",
    )(comb, results)


def solution(mesh):
    placed = (
        P(("parts", "expert", "tile"), None),
        P(("parts", "expert", "tile"), None),
        P(("parts", "expert", "tile"), None),
        P("expert", None, "tile"),
        P("expert", None, "tile"),
        P("expert", "tile", None),
    )
    return jax.shard_map(
        shards,
        mesh=mesh,
        in_specs=placed,
        out_specs=P(("parts", "expert", "tile"), None),
        check_vma=False,
    )
```
